128 devices in a mesh: col: 16 (over x, y_hi, core), row: 8 (over z, y_lo).
Axes of the slice: x: 4, y: 4 (y_hi: 2, y_lo: 2; y = y_hi * 2 + y_lo), z: 4, core: 2. Of those that a mesh axis runs over, the one named last changes fastest.
Arguments:
- matrix: float32 [28672, 8192], P('row', 'col'), may hold values from -6 to 6
- vectors: float32 [8192, 8192], P('row', 'col'), may hold values from -6 to 6
Outputs:
- next_matrix: float32 [28672, 8192], P('row', 'col')
- next_vectors: float32 [8192, 8192], P('row', 'col')
The draws below stay inside these ranges and needn't reach their ends.
All inputs are finite; a program needn't handle non-finite values.
Results may differ from the reference program's by a relative error of at most 0.0003.
Values sent between devices are 32-bit elements; how exact they have to be, the bound alone decides.
No kernel may reach another device: no remote copies, remote signals or barrier semaphores. Data moves between devices by JAX's collectives and lax.ppermute only.
A program may use at most 128 MiB of HBM per device.

```python
import jax
import jax.numpy as jnp
from jax import lax

BLOCK_COLS = 256
POLAR_STEPS = 10
ALL_ROWS = 28672
ALL_COLS = 8192
N_COL = 16


def block_levels(key, extent, cuts, smallest, largest):
    def one(position, blocks):
        heights = jax.random.uniform(jax.random.fold_in(jax.random.fold_in(key, 6), position), (blocks,), jnp.float32, smallest / len(cuts), largest / len(cuts))
        return jnp.repeat(jnp.exp(heights), extent[position] // blocks).reshape((-1,) + (1,) * (len(extent) - position - 1))

    gain = one(*cuts[0])
    for cut in cuts[1:]:
        gain = gain * one(*cut)
    return gain


def scatter_about(rng, shape, width, bound, split=(), kind=jnp.bfloat16):
    values = jax.random.normal(rng, shape, jnp.float32) * width
    if len(split) > 0:
        values = block_levels(rng, shape, split, -0.22, 0.18) * values
    return jnp.clip(values, min=-bound, max=bound).astype(kind)


def setup_inputs(seed: int = 0) -> dict:
    streams_of = jax.random.split(jax.random.key(seed), 3)
    matrix = scatter_about(streams_of[0], (ALL_ROWS, ALL_COLS), 1.0, 6.0, ((0, 8), (1, 16)), jnp.float32)
    vectors = scatter_about(streams_of[1], (ALL_COLS, ALL_COLS), 1.0, 6.0, ((0, 8), (1, 16)), jnp.float32)
    return {"matrix": matrix, "vectors": vectors}


def make_transform(gram):
    highest = lax.Precision.HIGHEST
    lower = jnp.linalg.cholesky(gram)
    ident = jnp.eye(gram.shape[0], dtype=gram.dtype)
    inverse = jax.scipy.linalg.solve_triangular(lower, ident, lower=True)
    start = inverse.T * jnp.diagonal(lower)[None, :]
    magnitude = jnp.abs(start)
    spectral_bound = jnp.sqrt(jnp.max(lax.optimization_barrier(jnp.sum(magnitude, axis=0))) * jnp.max(lax.optimization_barrier(jnp.sum(magnitude, axis=1))))
    approx = start / spectral_bound
    for step in range(POLAR_STEPS):
        square = jnp.dot(approx.T.astype(jnp.float32), approx.astype(jnp.float32), precision=highest, preferred_element_type=jnp.float32)
        approx = 1.5 * approx - 0.5 * jnp.dot(approx.astype(jnp.float32), square.astype(jnp.float32), precision=highest, preferred_element_type=jnp.float32)
    return approx

def arrange(stacked):
    tops = stacked[:, :, :BLOCK_COLS]
    bottoms = stacked[:, :, BLOCK_COLS:]
    new_tops = jnp.concatenate([tops[0:1], bottoms[0:1], tops[1:N_COL - 1]], axis=0)
    new_bottoms = jnp.concatenate([bottoms[1:], tops[N_COL - 1:]], axis=0)
    joined = jnp.concatenate([new_tops, new_bottoms], axis=2)
    return jnp.transpose(joined, (1, 0, 2)).reshape(stacked.shape[1], N_COL * 2 * BLOCK_COLS)

def reference(matrix, vectors):
    width_pair = 2 * BLOCK_COLS
    highest = lax.Precision.HIGHEST

    def one_pair(index):
        start = (index * width_pair).astype(jnp.int32)
        block = lax.dynamic_slice_in_dim(matrix, start, width_pair, 1)
        factor = lax.dynamic_slice_in_dim(vectors, start, width_pair, 1)
        gram = jnp.dot(block.T.astype(jnp.float32), block.astype(jnp.float32), precision=highest, preferred_element_type=jnp.float32)
        transform = make_transform(gram)
        moved = jnp.dot(block.astype(jnp.float32), transform.astype(jnp.float32), precision=highest, preferred_element_type=jnp.float32)
        turned = jnp.dot(factor.astype(jnp.float32), transform.astype(jnp.float32), precision=highest, preferred_element_type=jnp.float32)
        return (moved, turned)
    moved, turned = lax.map(one_pair, jnp.arange(N_COL, dtype=jnp.int32))
    return (arrange(moved), arrange(turned))
```

```python
import functools

import jax
import jax.numpy as jnp
from jax import lax
from jax.experimental import pallas as pl
from jax.experimental.pallas import tpu as pltpu
from jax.sharding import PartitionSpec as P

POLAR_STEPS = 10
LEAF = 128
F32 = jnp.float32
BF16 = jnp.bfloat16
NT = (((1,), (1,)), ((), ()))
NN = (((1,), (0,)), ((), ()))
TN = (((0,), (0,)), ((), ()))


def split(x):
    hi = x.astype(BF16)
    return hi, (x - hi.astype(F32)).astype(BF16)


def dot3(a, b, dims=NN):
    dot = functools.partial(lax.dot_general, dimension_numbers=dims, preferred_element_type=F32)
    return dot(a[0], b[1]) + dot(a[1], b[0]) + dot(a[0], b[0])


def dot_high(a, b, dims=NN):
    return lax.dot_general(a, b, dims, precision=lax.Precision.HIGHEST, preferred_element_type=F32)


def eliminate_leaf(block):
    groups = LEAF // 8
    rows = [block[8 * g : 8 * g + 8, :] for g in range(groups)]
    inv_pivot = []
    lane = lax.broadcasted_iota(jnp.int32, (8, LEAF), 1)
    sub = lax.broadcasted_iota(jnp.int32, (8, LEAF), 0)
    for p in range(groups):
        j0 = 8 * p
        panel = rows[p]
        cols = [jnp.broadcast_to(panel[:, j0 + u : j0 + u + 1], (8, LEAF)) for u in range(8)]
        s = [[None] * 8 for _ in range(8)]
        for t in range(8):
            for u in range(t, 8):
                s[t][u] = jnp.broadcast_to(cols[u][t : t + 1, :], (8, LEAF))
        in_panel = (lane >= j0) & (lane < j0 + 8)
        unit = (lane - j0 == sub).astype(F32)
        panel = jnp.where(in_panel, unit, panel)
        line = [jnp.broadcast_to(panel[t : t + 1, :], (8, LEAF)) for t in range(8)]
        recip = []
        for t in range(8):
            r = 1.0 / s[t][t]
            recip.append(r)
            for u in range(t + 1, 8):
                f = s[t][u] * r
                for v in range(u, 8):
                    s[u][v] = s[u][v] - f * s[t][v]
                line[u] = line[u] - f * line[t]
        done = line[7]
        inv = recip[7]
        for t in range(6, -1, -1):
            done = jnp.where(sub == t, line[t], done)
            inv = jnp.where(sub == t, recip[t], inv)
        rows[p] = done
        inv_pivot.append(inv)
        for g in range(p + 1, groups):
            cur = rows[g]
            left = [jnp.broadcast_to(cur[:, j0 + u : j0 + u + 1], (8, LEAF)) for u in range(8)]
            cur = jnp.where(in_panel, 0.0, cur)
            for t in range(8):
                m = left[t] * recip[t]
                for u in range(t + 1, 8):
                    left[u] = left[u] - m * s[t][u]
                cur = cur - m * line[t]
            rows[g] = cur
    return jnp.concatenate(rows, axis=0), jnp.concatenate(inv_pivot, axis=0)


def gram_kernel(x_ref, out_ref, same, cross):
    step = pl.program_id(0)
    half = x_ref.shape[1] // 2

    @pl.when(step == 0)
    def _():
        same[...] = jnp.zeros_like(same)
        cross[...] = jnp.zeros_like(cross)

    hi, lo = split(x_ref[...])
    dot = functools.partial(lax.dot_general, dimension_numbers=TN, preferred_element_type=F32)
    same[:half, :] += dot(hi[:, :half], hi)
    same[half:, half:] += dot(hi[:, half:], hi[:, half:])
    cross[...] += dot(hi, lo)

    @pl.when(step == pl.num_programs(0) - 1)
    def _():
        out_ref[:half] = same[:half, :half] + (cross[:half, :half] + cross[:half, :half].T)
        out_ref[half : 2 * half] = same[:half, half:] + (cross[:half, half:] + cross[half:, :half].T)
        out_ref[2 * half :] = same[half:, half:] + (cross[half:, half:] + cross[half:, half:].T)


def make_gram(x, tile=512):
    rows, n = x.shape
    half = n // 2
    return pl.pallas_call(
        gram_kernel,
        grid=(rows // tile,),
        out_shape=jax.ShapeDtypeStruct((3 * half, half), F32),
        in_specs=[pl.BlockSpec((tile, n), lambda i: (i, 0))],
        out_specs=pl.BlockSpec((3 * half, half), lambda i: (0, 0)),
        scratch_shapes=[pltpu.VMEM((n, n), F32), pltpu.VMEM((n, n), F32)],
        compiler_params=pltpu.CompilerParams(vmem_limit_bytes=32 * 2**20),
    )(x)


def sum_over_rows(gram):
    count = lax.axis_size("row")
    pieces = gram.reshape(count, gram.shape[0] // count, gram.shape[1])
    theirs = lax.all_to_all(pieces, "row", 0, 0, tiled=True)
    own = jnp.sum(theirs, axis=0)
    spread = jnp.broadcast_to(own[None], pieces.shape)
    return lax.all_to_all(spread, "row", 0, 0, tiled=True).reshape(gram.shape)


def transform_kernel(swap_ref, gram_ref, hi_ref, lo_ref, work):
    n = work.shape[0]
    half = n // 2
    work[:half, :half] = gram_ref[:half]
    work[:half, half:] = gram_ref[half : 2 * half]
    work[half:, :half] = gram_ref[half : 2 * half].T
    work[half:, half:] = gram_ref[2 * half :]

    def block_step(p, carry):
        at = pl.ds(pl.multiple_of(p * LEAF, LEAF), LEAF)
        block, inv = eliminate_leaf(work[at, at])
        r = lax.broadcasted_iota(jnp.int32, (LEAF, LEAF), 0)
        c = lax.broadcasted_iota(jnp.int32, (LEAF, LEAF), 1)
        lower = jnp.where(c <= r, block, 0.0)
        work[at, at] = (r == c).astype(F32)
        panel = dot_high(lower, work[at, :])
        col = lax.broadcasted_iota(jnp.int32, (LEAF, n), 1)
        scaled = jnp.where(col >= (p + 1) * LEAF, panel * inv[:, :1], 0.0)
        work[at, :] = panel
        later = lax.broadcasted_iota(jnp.int32, (n, LEAF), 0) >= (p + 1) * LEAF
        work[:, at] = jnp.where(later, 0.0, work[:, at])
        work[...] -= dot_high(scaled, panel, TN)
        return carry

    lax.fori_loop(0, n // LEAF, block_step, 0)
    r = lax.broadcasted_iota(jnp.int32, (n, n), 0)
    c = lax.broadcasted_iota(jnp.int32, (n, n), 1)
    start = jnp.where(c <= r, work[...], 0.0)
    mag = jnp.abs(start)
    bound = jnp.sqrt(jnp.max(jnp.sum(mag, axis=0, keepdims=True)) * jnp.max(jnp.sum(mag, axis=1, keepdims=True)))
    work[...] = start / bound

    def polar_step(k, carry):
        z = work[...]
        zs = split(z)
        g = dot3(zs, zs, NT)
        work[...] = 1.5 * z - 0.5 * dot3(split(g), zs)
        return carry

    lax.fori_loop(0, POLAR_STEPS, polar_step, 0)
    for side in range(2):
        begin = pl.multiple_of(jnp.bitwise_xor(swap_ref[0], side) * half, half)
        hi, lo = split(work[pl.ds(begin, half), :].T)
        hi_ref[:, side * half : (side + 1) * half] = hi
        lo_ref[:, side * half : (side + 1) * half] = lo


def make_transform(gram, swap):
    n = 2 * gram.shape[1]
    return pl.pallas_call(
        transform_kernel,
        out_shape=[jax.ShapeDtypeStruct((n, n), BF16)] * 2,
        in_specs=[pl.BlockSpec(memory_space=pltpu.SMEM), pl.BlockSpec(memory_space=pltpu.VMEM)],
        out_specs=[pl.BlockSpec(memory_space=pltpu.VMEM)] * 2,
        scratch_shapes=[pltpu.VMEM((n, n), F32)],
        compiler_params=pltpu.CompilerParams(vmem_limit_bytes=48 * 2**20),
    )(swap, gram)


def apply_kernel(x_ref, hi_ref, lo_ref, up_ref, down_ref):
    half = up_ref.shape[1]
    xs = split(x_ref[...])
    both = dot3(xs, (hi_ref[...], lo_ref[...]))
    up_ref[...] = both[:, :half]
    down_ref[...] = both[:, half:]


def apply_rows(x, begin, rows, parts, tile=512):
    n = x.shape[1]
    half = n // 2
    first = begin // tile
    return pl.pallas_call(
        apply_kernel,
        grid=(rows // tile,),
        out_shape=[jax.ShapeDtypeStruct((rows, half), F32)] * 2,
        in_specs=[
            pl.BlockSpec((tile, n), lambda i: (first + i, 0)),
            pl.BlockSpec((n, n), lambda i: (0, 0)),
            pl.BlockSpec((n, n), lambda i: (0, 0)),
        ],
        out_specs=[pl.BlockSpec((tile, half), lambda i: (i, 0))] * 2,
        compiler_params=pltpu.CompilerParams(vmem_limit_bytes=32 * 2**20),
        cost_estimate=pl.CostEstimate(flops=6 * rows * n * n, bytes_accessed=8 * rows * n, transcendentals=0),
    )(x, *parts)


def place_kernel(begin, ends_ref, from_left, from_right, own_up, own_down, *rest):
    out, sems = rest[-2], rest[-1]
    rows, half = from_left.shape
    at = pl.ds(begin, rows)
    for side, (own, other) in enumerate(((own_down, from_left), (own_up, from_right))):
        target = out.at[at, pl.ds(side * half, half)]

        @pl.when(ends_ref[side] == 1)
        def _():
            pltpu.make_async_copy(own, target, sems.at[side]).start()

        @pl.when(ends_ref[side] == 0)
        def _():
            pltpu.make_async_copy(other, target, sems.at[side]).start()

    for side in range(2):
        target = out.at[at, pl.ds(side * half, half)]
        pltpu.make_async_copy(from_left, target, sems.at[side]).wait()


def place_rows(out, shape, begin, ends, blocks):
    args = [ends, *blocks] + ([] if out is None else [out])
    return pl.pallas_call(
        functools.partial(place_kernel, begin),
        out_shape=jax.ShapeDtypeStruct(shape, F32),
        in_specs=[pl.BlockSpec(memory_space=pltpu.SMEM)] + [pl.BlockSpec(memory_space=pl.ANY)] * (len(args) - 1),
        out_specs=pl.BlockSpec(memory_space=pl.ANY),
        scratch_shapes=[pltpu.SemaphoreType.DMA((2,))],
        input_output_aliases={} if out is None else {len(args) - 1: 0},
    )(*args)


CHUNKS = ((0, 0, 512), (0, 512, 1024), (0, 1536, 1024), (1, 0, 1024), (0, 2560, 1024))


def on_device(matrix, vectors):
    count_col = lax.axis_size("col")
    own_index = lax.axis_index("col")
    ends = jnp.stack([own_index == 0, own_index == count_col - 1]).astype(jnp.int32)
    upward = [(i, i + 1) for i in range(count_col - 1)]
    downward = [(i + 1, i) for i in range(count_col - 1)]
    sources = (matrix, vectors)
    results = [None, None]
    gram = sum_over_rows(make_gram(matrix))
    parts = make_transform(gram, ends)
    for which, begin, rows in CHUNKS:
        up, down = apply_rows(sources[which], begin, rows, parts)
        from_left = lax.ppermute(up, "col", upward)
        from_right = lax.ppermute(down, "col", downward)
        results[which] = place_rows(
            results[which], sources[which].shape, begin, ends, (from_left, from_right, up, down)
        )
    return tuple(results)


def solution(mesh):
    in_specs = (P("row", "col"), P("row", "col"))
    out_specs = (P("row", "col"), P("row", "col"))
    return jax.shard_map(
        on_device, mesh=mesh, in_specs=in_specs, out_specs=out_specs, check_vma=False
    )
```

```python
import functools

import jax
import jax.numpy as jnp
from jax import lax
from jax.experimental import pallas as pl
from jax.experimental.pallas import tpu as pltpu
from jax.sharding import PartitionSpec as P

POLAR_STEPS = 10
LEAF = 128
VMEM_ALL = 60 * 2**20
F32 = jnp.float32
BF16 = jnp.bfloat16
NT = (((1,), (1,)), ((), ()))
NN = (((1,), (0,)), ((), ()))
TN = (((0,), (0,)), ((), ()))


def split(x):
    hi = x.astype(BF16)
    return hi, (x - hi.astype(F32)).astype(BF16)


def dot3(a, b, dims=NN):
    dot = functools.partial(lax.dot_general, dimension_numbers=dims, preferred_element_type=F32)
    return dot(a[0], b[1]) + dot(a[1], b[0]) + dot(a[0], b[0])


def dot_high(a, b, dims=NN):
    return lax.dot_general(a, b, dims, precision=lax.Precision.HIGHEST, preferred_element_type=F32)


def eliminate_leaf(block):
    groups = LEAF // 8
    rows = [block[8 * g : 8 * g + 8, :] for g in range(groups)]
    inv_pivot = []
    lane = lax.broadcasted_iota(jnp.int32, (8, LEAF), 1)
    sub = lax.broadcasted_iota(jnp.int32, (8, LEAF), 0)
    for p in range(groups):
        j0 = 8 * p
        panel = rows[p]
        cols = [jnp.broadcast_to(panel[:, j0 + u : j0 + u + 1], (8, LEAF)) for u in range(8)]
        s = [[None] * 8 for _ in range(8)]
        for t in range(8):
            for u in range(t, 8):
                s[t][u] = jnp.broadcast_to(cols[u][t : t + 1, :], (8, LEAF))
        in_panel = (lane >= j0) & (lane < j0 + 8)
        unit = (lane - j0 == sub).astype(F32)
        panel = jnp.where(in_panel, unit, panel)
        line = [jnp.broadcast_to(panel[t : t + 1, :], (8, LEAF)) for t in range(8)]
        recip = []
        for t in range(8):
            r = 1.0 / s[t][t]
            recip.append(r)
            for u in range(t + 1, 8):
                f = s[t][u] * r
                for v in range(u, 8):
                    s[u][v] = s[u][v] - f * s[t][v]
                line[u] = line[u] - f * line[t]
        done = line[7]
        inv = recip[7]
        for t in range(6, -1, -1):
            done = jnp.where(sub == t, line[t], done)
            inv = jnp.where(sub == t, recip[t], inv)
        rows[p] = done
        inv_pivot.append(inv)
        for g in range(p + 1, groups):
            cur = rows[g]
            left = [jnp.broadcast_to(cur[:, j0 + u : j0 + u + 1], (8, LEAF)) for u in range(8)]
            cur = jnp.where(in_panel, 0.0, cur)
            for t in range(8):
                m = left[t] * recip[t]
                for u in range(t + 1, 8):
                    left[u] = left[u] - m * s[t][u]
                cur = cur - m * line[t]
            rows[g] = cur
    return jnp.concatenate(rows, axis=0), jnp.concatenate(inv_pivot, axis=0)


def gram_kernel(x_ref, out_ref, same, cross):
    step = pl.program_id(0)
    half = x_ref.shape[1] // 2

    @pl.when(step == 0)
    def _():
        same[...] = jnp.zeros_like(same)
        cross[...] = jnp.zeros_like(cross)

    hi, lo = split(x_ref[...])
    dot = functools.partial(lax.dot_general, dimension_numbers=TN, preferred_element_type=F32)
    same[:half, :] += dot(hi[:, :half], hi)
    same[half:, half:] += dot(hi[:, half:], hi[:, half:])
    cross[...] += dot(hi, lo)

    @pl.when(step == pl.num_programs(0) - 1)
    def _():
        out_ref[:half] = same[:half, :half] + (cross[:half, :half] + cross[:half, :half].T)
        out_ref[half : 2 * half] = same[:half, half:] + (cross[:half, half:] + cross[half:, :half].T)
        out_ref[2 * half :] = same[half:, half:] + (cross[half:, half:] + cross[half:, half:].T)


def make_gram(x, tile=512):
    rows, n = x.shape
    half = n // 2
    return pl.pallas_call(
        gram_kernel,
        grid=(rows // tile,),
        out_shape=jax.ShapeDtypeStruct((3 * half, half), F32),
        in_specs=[pl.BlockSpec((tile, n), lambda i: (i, 0))],
        out_specs=pl.BlockSpec((3 * half, half), lambda i: (0, 0)),
        scratch_shapes=[pltpu.VMEM((n, n), F32), pltpu.VMEM((n, n), F32)],
        compiler_params=pltpu.CompilerParams(vmem_limit_bytes=14 * 2**20),
        cost_estimate=pl.CostEstimate(flops=1024, bytes_accessed=1024, transcendentals=0),
    )(x)


def sum_over_rows(gram):
    count = lax.axis_size("row")
    pieces = gram.reshape(count, gram.shape[0] // count, gram.shape[1])
    theirs = lax.all_to_all(pieces, "row", 0, 0, tiled=True)
    own = jnp.sum(theirs, axis=0)
    spread = jnp.broadcast_to(own[None], pieces.shape)
    return lax.all_to_all(spread, "row", 0, 0, tiled=True).reshape(gram.shape)


def transform_kernel(swap_ref, gram_ref, inner_ref, outer_ref, work):
    n = work.shape[0]
    half = n // 2
    work[:half, :half] = gram_ref[:half]
    work[:half, half:] = gram_ref[half : 2 * half]
    work[half:, :half] = gram_ref[half : 2 * half].T
    work[half:, half:] = gram_ref[2 * half :]

    def block_step(p, carry):
        at = pl.ds(pl.multiple_of(p * LEAF, LEAF), LEAF)
        block, inv = eliminate_leaf(work[at, at])
        r = lax.broadcasted_iota(jnp.int32, (LEAF, LEAF), 0)
        c = lax.broadcasted_iota(jnp.int32, (LEAF, LEAF), 1)
        lower = jnp.where(c <= r, block, 0.0)
        work[at, at] = (r == c).astype(F32)
        for q in range(n // LEAF):

            @pl.when(p == q)
            def _():
                e = (q + 1) * LEAF
                panel = dot_high(lower, work[q * LEAF : e, :])
                work[q * LEAF : e, :] = panel
                if e < n:
                    scaled = panel[:, e:] * inv[:, :1]
                    work[e:, q * LEAF : e] = jnp.zeros((n - e, LEAF), F32)
                    work[e:, :] -= dot_high(scaled, panel, TN)

        return carry

    lax.fori_loop(0, n // LEAF, block_step, 0)
    r = lax.broadcasted_iota(jnp.int32, (n, n), 0)
    c = lax.broadcasted_iota(jnp.int32, (n, n), 1)
    start = jnp.where(c <= r, work[...], 0.0)
    mag = jnp.abs(start)
    bound = jnp.sqrt(jnp.max(jnp.sum(mag, axis=0, keepdims=True)) * jnp.max(jnp.sum(mag, axis=1, keepdims=True)))
    work[...] = start / bound

    def polar_step(k, carry):
        z = work[...]
        zs = split(z)
        g = dot3(zs, zs, NT)
        work[...] = 1.5 * z - 0.5 * dot3(split(g), zs)
        return carry

    lax.fori_loop(0, POLAR_STEPS, polar_step, 0)
    for side, out in enumerate((inner_ref, outer_ref)):
        begin = pl.multiple_of(jnp.bitwise_xor(swap_ref[0], side) * half, half)
        out[...] = work[pl.ds(begin, half), :].T


def make_transform(gram, swap):
    n = 2 * gram.shape[1]
    return pl.pallas_call(
        transform_kernel,
        out_shape=[jax.ShapeDtypeStruct((n, n // 2), F32)] * 2,
        in_specs=[pl.BlockSpec(memory_space=pltpu.SMEM), pl.BlockSpec(memory_space=pltpu.VMEM)],
        out_specs=[pl.BlockSpec(memory_space=pltpu.VMEM)] * 2,
        scratch_shapes=[pltpu.VMEM((n, n), F32)],
        compiler_params=pltpu.CompilerParams(vmem_limit_bytes=16 * 2**20),
        cost_estimate=pl.CostEstimate(flops=1024, bytes_accessed=1024, transcendentals=0),
    )(swap, gram)


def apply_kernel(x_ref, t_inner, t_outer, inner_ref, outer_ref, parts):
    half = inner_ref.shape[1]

    @pl.when(pl.program_id(0) == 0)
    def _():
        for side, t in enumerate((t_inner, t_outer)):
            hi, lo = split(t[...])
            parts[0, :, side * half : (side + 1) * half] = hi
            parts[1, :, side * half : (side + 1) * half] = lo

    both = dot3(split(x_ref[...]), (parts[0], parts[1]))
    inner_ref[...] = both[:, :half]
    outer_ref[...] = both[:, half:]


def apply_rows(x, begin, rows, turns, tile=512):
    n = x.shape[1]
    half = n // 2
    first = begin // tile
    return pl.pallas_call(
        apply_kernel,
        grid=(rows // tile,),
        out_shape=[jax.ShapeDtypeStruct((rows, half), F32)] * 2,
        in_specs=[
            pl.BlockSpec((tile, n), lambda i: (first + i, 0)),
            pl.BlockSpec((n, half), lambda i: (0, 0)),
            pl.BlockSpec((n, half), lambda i: (0, 0)),
        ],
        out_specs=[pl.BlockSpec((tile, half), lambda i: (i, 0))] * 2,
        scratch_shapes=[pltpu.VMEM((2, n, n), BF16)],
        compiler_params=pltpu.CompilerParams(vmem_limit_bytes=14 * 2**20),
        cost_estimate=pl.CostEstimate(flops=6 * rows * n * n, bytes_accessed=8 * rows * n, transcendentals=0),
    )(x, *turns)


def arrived_kernel(core_ref, inner, outer, t_inner, t_outer, *rest):
    out, parts = rest[-2], rest[-1]
    half = t_inner.shape[1]

    @pl.when(pl.program_id(0) == 0)
    def _():
        for side, t in enumerate((t_inner, t_outer)):
            hi, lo = split(t[...])
            parts[side, 0] = hi
            parts[side, 1] = lo

    for side, block in enumerate((inner, outer)):
        at = pl.ds(pl.multiple_of(jnp.bitwise_xor(core_ref[0], 1 - side) * half, half), half)
        out[:, at] = dot3(split(block[...]), (parts[side, 0], parts[side, 1]))


def arrived_rows(out, shape, begin, rows, core, blocks, skip, turns, tile=512):
    n = shape[1]
    first, here = begin // tile, skip // tile
    args = [core, *blocks, *turns] + ([] if out is None else [out])
    return pl.pallas_call(
        arrived_kernel,
        grid=(rows // tile,),
        in_specs=[
            pl.BlockSpec(memory_space=pltpu.SMEM),
            pl.BlockSpec((tile, n), lambda i: (here + i, 0)),
            pl.BlockSpec((tile, n), lambda i: (here + i, 0)),
            pl.BlockSpec((n, n // 2), lambda i: (0, 0)),
            pl.BlockSpec((n, n // 2), lambda i: (0, 0)),
        ]
        + [pl.BlockSpec(memory_space=pl.ANY)] * (len(args) - 5),
        out_specs=pl.BlockSpec((tile, n), lambda i: (first + i, 0)),
        scratch_shapes=[pltpu.VMEM((2, 2, n, n // 2), BF16)],
        out_shape=jax.ShapeDtypeStruct(shape, F32),
        input_output_aliases={} if out is None else {len(args) - 1: 0},
        compiler_params=pltpu.CompilerParams(vmem_limit_bytes=24 * 2**20),
        cost_estimate=pl.CostEstimate(flops=6 * rows * n * n, bytes_accessed=8 * rows * n, transcendentals=0),
    )(*args)


def place_kernel(core_ref, inner, outer, *rest):
    out = rest[-1]
    half = inner.shape[1]
    for side, block in enumerate((inner, outer)):
        at = pl.ds(pl.multiple_of(jnp.bitwise_xor(core_ref[0], 1 - side) * half, half), half)
        out[:, at] = block[...]


def place_rows(out, shape, begin, core, blocks, tile=512):
    rows, half = blocks[0].shape
    first = begin // tile
    args = [core, *blocks] + ([] if out is None else [out])
    return pl.pallas_call(
        place_kernel,
        grid=(rows // tile,),
        in_specs=[pl.BlockSpec(memory_space=pltpu.SMEM)]
        + [pl.BlockSpec((tile, half), lambda i: (i, 0))] * 2
        + [pl.BlockSpec(memory_space=pl.ANY)] * (len(args) - 3),
        out_specs=pl.BlockSpec((tile, 2 * half), lambda i: (first + i, 0)),
        out_shape=jax.ShapeDtypeStruct(shape, F32),
        input_output_aliases={} if out is None else {len(args) - 1: 0},
        compiler_params=pltpu.CompilerParams(vmem_limit_bytes=8 * 2**20),
        cost_estimate=pl.CostEstimate(flops=1024, bytes_accessed=16 * rows * half, transcendentals=0),
    )(*args)


EARLY = ((1, 0, 1024),)
LATE = ((0, 0, 1024), (0, 1024, 1024), (0, 2048, 1024), (0, 3072, 512))


def raw_rows(sources):
    blocks = [lax.slice_in_dim(sources[w], begin, begin + rows) for w, begin, rows in EARLY]
    return blocks[0] if len(blocks) == 1 else jnp.concatenate(blocks)


def on_device(matrix, vectors):
    count = lax.axis_size("col")
    own_index = lax.axis_index("col")
    core = jnp.reshape(own_index % 2, (1,)).astype(jnp.int32)
    within = [(i, i ^ 1) for i in range(count)]
    across = [(0, 0), (count - 1, count - 1)]
    across += [(i, i + 1) for i in range(1, count - 1, 2)] + [(i + 1, i) for i in range(1, count - 1, 2)]
    swap = jnp.where(own_index == 0, 1, core).astype(jnp.int32)
    sources = (matrix, vectors)
    results = [None, None]

    def pass_on(inner, outer):
        return lax.ppermute(inner, "col", within), lax.ppermute(outer, "col", across)

    gram = sum_over_rows(make_gram(matrix))
    raw, gram = lax.optimization_barrier((raw_rows(sources), gram))
    early = pass_on(raw, raw)
    own_turns = make_transform(gram, swap)
    waits = [early, pass_on(*own_turns)]
    for which, begin, rows in LATE:
        blocks = apply_rows(sources[which], begin, rows, own_turns)
        blocks, waits[-2] = lax.optimization_barrier((blocks, waits[-2]))
        waits.append(pass_on(*blocks))
    early, turns = waits[:2]
    skip = 0
    for which, begin, rows in EARLY:
        results[which] = arrived_rows(
            results[which], sources[which].shape, begin, rows, core, early, skip, turns
        )
        skip += rows
    for (which, begin, rows), blocks in zip(LATE, waits[2:]):
        results[which] = place_rows(results[which], sources[which].shape, begin, core, blocks)
    return tuple(results)


def solution(mesh):
    in_specs = (P("row", "col"), P("row", "col"))
    out_specs = (P("row", "col"), P("row", "col"))
    return jax.shard_map(
        on_device, mesh=mesh, in_specs=in_specs, out_specs=out_specs, check_vma=False
    )
```

```python
import functools

import jax
import jax.numpy as jnp
from jax import lax
from jax.experimental import pallas as pl
from jax.experimental.pallas import tpu as pltpu
from jax.sharding import PartitionSpec as P

POLAR_STEPS = 10
LEAF = 128
VMEM_ALL = 60 * 2**20
BLOCKS = 4
UPPER = tuple((i, j) for i in range(BLOCKS) for j in range(i, BLOCKS))
PIECES = 4
DEPTH = 2
F32 = jnp.float32
BF16 = jnp.bfloat16
NT = (((1,), (1,)), ((), ()))
NN = (((1,), (0,)), ((), ()))
TN = (((0,), (0,)), ((), ()))


def split(x):
    hi = x.astype(BF16)
    return hi, (x - hi.astype(F32)).astype(BF16)


def dot3(a, b, dims=NN):
    dot = functools.partial(lax.dot_general, dimension_numbers=dims, preferred_element_type=F32)
    return dot(a[0], b[1]) + dot(a[1], b[0]) + dot(a[0], b[0])


def dot_high(a, b, dims=NN):
    return lax.dot_general(a, b, dims, precision=lax.Precision.HIGHEST, preferred_element_type=F32)


def eliminate_leaf(block):
    groups = LEAF // 8
    rows = [block[8 * g : 8 * g + 8, :] for g in range(groups)]
    inv_pivot = []
    lane = lax.broadcasted_iota(jnp.int32, (8, LEAF), 1)
    sub = lax.broadcasted_iota(jnp.int32, (8, LEAF), 0)
    for p in range(groups):
        j0 = 8 * p
        panel = rows[p]
        cols = [jnp.broadcast_to(panel[:, j0 + u : j0 + u + 1], (8, LEAF)) for u in range(8)]
        s = [[None] * 8 for _ in range(8)]
        for t in range(8):
            for u in range(t, 8):
                s[t][u] = jnp.broadcast_to(cols[u][t : t + 1, :], (8, LEAF))
        in_panel = (lane >= j0) & (lane < j0 + 8)
        unit = (lane - j0 == sub).astype(F32)
        panel = jnp.where(in_panel, unit, panel)
        line = [jnp.broadcast_to(panel[t : t + 1, :], (8, LEAF)) for t in range(8)]
        recip = []
        for t in range(8):
            r = 1.0 / s[t][t]
            recip.append(r)
            for u in range(t + 1, 8):
                f = s[t][u] * r
                for v in range(u, 8):
                    s[u][v] = s[u][v] - f * s[t][v]
                line[u] = line[u] - f * line[t]
        done = line[7]
        inv = recip[7]
        for t in range(6, -1, -1):
            done = jnp.where(sub == t, line[t], done)
            inv = jnp.where(sub == t, recip[t], inv)
        rows[p] = done
        inv_pivot.append(inv)
        for g in range(p + 1, groups):
            cur = rows[g]
            left = [jnp.broadcast_to(cur[:, j0 + u : j0 + u + 1], (8, LEAF)) for u in range(8)]
            cur = jnp.where(in_panel, 0.0, cur)
            for t in range(8):
                m = left[t] * recip[t]
                for u in range(t + 1, 8):
                    left[u] = left[u] - m * s[t][u]
                cur = cur - m * line[t]
            rows[g] = cur
    return jnp.concatenate(rows, axis=0), jnp.concatenate(inv_pivot, axis=0)


def gram_kernel(cuts, x_hbm, out_ref, x, same, cross, sems):
    half = x.shape[1] // 2
    copies = []
    for k, (begin, end) in enumerate(zip(cuts[:-1], cuts[1:])):
        at = pl.ds(begin, end - begin)
        copies.append(pltpu.make_async_copy(x_hbm.at[at], x.at[at], sems.at[k]))
        copies[-1].start()
    dot = functools.partial(lax.dot_general, dimension_numbers=TN, preferred_element_type=F32)
    for k, (begin, end) in enumerate(zip(cuts[:-1], cuts[1:])):
        copies[k].wait()
        hi, lo = split(x[begin:end])
        first, last, mixed = dot(hi[:, :half], hi), dot(hi[:, half:], hi[:, half:]), dot(hi, lo)
        if k == 0:
            same[:half, :] = first
            same[half:, half:] = last
            cross[...] = mixed
        else:
            same[:half, :] += first
            same[half:, half:] += last
            cross[...] += mixed
    for k, (i, j) in enumerate(UPPER):
        rows, cols = slice(i * LEAF, (i + 1) * LEAF), slice(j * LEAF, (j + 1) * LEAF)
        out_ref[k * LEAF : (k + 1) * LEAF] = same[rows, cols] + (cross[rows, cols] + cross[cols, rows].T)


def make_gram(x):
    rows, n = x.shape
    size = (len(UPPER) * LEAF, LEAF)
    cuts = (0, rows // 7, 3 * rows // 7, rows)
    return pl.pallas_call(
        functools.partial(gram_kernel, cuts),
        out_shape=jax.ShapeDtypeStruct(size, F32),
        in_specs=[pl.BlockSpec(memory_space=pl.ANY)],
        out_specs=pl.BlockSpec(memory_space=pltpu.VMEM),
        scratch_shapes=[
            pltpu.VMEM((rows, n), F32),
            pltpu.VMEM((n, n), F32),
            pltpu.VMEM((n, n), F32),
            pltpu.SemaphoreType.DMA((len(cuts) - 1,)),
        ],
        compiler_params=pltpu.CompilerParams(vmem_limit_bytes=VMEM_ALL),
        cost_estimate=pl.CostEstimate(flops=1024, bytes_accessed=1024, transcendentals=0),
    )(x)


def add_kernel(pieces, out_ref):
    total = pieces[0]
    for k in range(1, pieces.shape[0]):
        total = total + pieces[k]
    for k in range(pieces.shape[0]):
        out_ref[k] = total


def sum_over_rows(gram):
    count = lax.axis_size("row")
    pieces = gram.reshape(count, gram.shape[0] // count, gram.shape[1])
    theirs = lax.all_to_all(pieces, "row", 0, 0, tiled=True)
    spread = pl.pallas_call(
        add_kernel,
        out_shape=jax.ShapeDtypeStruct(pieces.shape, F32),
        in_specs=[pl.BlockSpec(memory_space=pltpu.VMEM)],
        out_specs=pl.BlockSpec(memory_space=pltpu.VMEM),
        compiler_params=pltpu.CompilerParams(vmem_limit_bytes=8 * 2**20),
        cost_estimate=pl.CostEstimate(flops=1024, bytes_accessed=1024, transcendentals=0),
    )(theirs)
    return lax.all_to_all(spread, "row", 0, 0, tiled=True).reshape(gram.shape)


def transform_kernel(swap_ref, gram_ref, inner_ref, outer_ref, work):
    n = work.shape[0]
    half = n // 2
    for k, (i, j) in enumerate(UPPER):
        block = gram_ref[k * LEAF : (k + 1) * LEAF]
        work[i * LEAF : (i + 1) * LEAF, j * LEAF : (j + 1) * LEAF] = block
        if i != j:
            work[j * LEAF : (j + 1) * LEAF, i * LEAF : (i + 1) * LEAF] = block.T

    def block_step(p, carry):
        at = pl.ds(pl.multiple_of(p * LEAF, LEAF), LEAF)
        block, inv = eliminate_leaf(work[at, at])
        r = lax.broadcasted_iota(jnp.int32, (LEAF, LEAF), 0)
        c = lax.broadcasted_iota(jnp.int32, (LEAF, LEAF), 1)
        lower = jnp.where(c <= r, block, 0.0)
        work[at, at] = (r == c).astype(F32)
        for q in range(n // LEAF):

            @pl.when(p == q)
            def _():
                e = (q + 1) * LEAF
                panel = dot_high(lower, work[q * LEAF : e, :])
                work[q * LEAF : e, :] = panel
                if e < n:
                    scaled = panel[:, e:] * inv[:, :1]
                    work[e:, q * LEAF : e] = jnp.zeros((n - e, LEAF), F32)
                    work[e:, :] -= dot_high(scaled, panel, TN)

        return carry

    lax.fori_loop(0, n // LEAF, block_step, 0)
    r = lax.broadcasted_iota(jnp.int32, (n, n), 0)
    c = lax.broadcasted_iota(jnp.int32, (n, n), 1)
    start = jnp.where(c <= r, work[...], 0.0)
    mag = jnp.abs(start)
    bound = jnp.sqrt(jnp.max(jnp.sum(mag, axis=0, keepdims=True)) * jnp.max(jnp.sum(mag, axis=1, keepdims=True)))
    work[...] = start / bound

    def polar_step(k, carry):
        z = work[...]
        zs = split(z)
        g = dot3(zs, zs, NT)
        work[...] = 1.5 * z - 0.5 * dot3(split(g), zs)
        return carry

    lax.fori_loop(0, POLAR_STEPS, polar_step, 0)
    for side, out in enumerate((inner_ref, outer_ref)):
        begin = pl.multiple_of(jnp.bitwise_xor(swap_ref[0], side) * half, half)
        out[...] = work[pl.ds(begin, half), :].T


def make_transform(gram, swap):
    n = BLOCKS * LEAF
    return pl.pallas_call(
        transform_kernel,
        out_shape=[jax.ShapeDtypeStruct((n, n // 2), F32)] * 2,
        in_specs=[pl.BlockSpec(memory_space=pltpu.SMEM), pl.BlockSpec(memory_space=pltpu.VMEM)],
        out_specs=[pl.BlockSpec(memory_space=pltpu.VMEM)] * 2,
        scratch_shapes=[pltpu.VMEM((n, n), F32)],
        compiler_params=pltpu.CompilerParams(vmem_limit_bytes=16 * 2**20),
        cost_estimate=pl.CostEstimate(flops=1024, bytes_accessed=1024, transcendentals=0),
    )(swap, gram)


def tile_for(*extents):
    return 512 if all(e % 512 == 0 for e in extents) else 256


def apply_kernel(x_ref, t_inner, t_outer, inner_ref, outer_ref, parts):
    half = inner_ref.shape[1]

    @pl.when(pl.program_id(0) == 0)
    def _():
        for side, t in enumerate((t_inner, t_outer)):
            hi, lo = split(t[...])
            parts[0, :, side * half : (side + 1) * half] = hi
            parts[1, :, side * half : (side + 1) * half] = lo

    both = dot3(split(x_ref[...]), (parts[0], parts[1]))
    inner_ref[...] = both[:, :half]
    outer_ref[...] = both[:, half:]


def apply_rows(x, begin, rows, turns):
    tile = tile_for(begin, rows)
    n = x.shape[1]
    half = n // 2
    first = begin // tile
    return pl.pallas_call(
        apply_kernel,
        grid=(rows // tile,),
        out_shape=[jax.ShapeDtypeStruct((rows, half), F32)] * 2,
        in_specs=[
            pl.BlockSpec((tile, n), lambda i: (first + i, 0)),
            pl.BlockSpec((n, half), lambda i: (0, 0)),
            pl.BlockSpec((n, half), lambda i: (0, 0)),
        ],
        out_specs=[pl.BlockSpec((tile, half), lambda i: (i, 0))] * 2,
        scratch_shapes=[pltpu.VMEM((2, n, n), BF16)],
        compiler_params=pltpu.CompilerParams(vmem_limit_bytes=14 * 2**20),
        cost_estimate=pl.CostEstimate(flops=6 * rows * n * n, bytes_accessed=8 * rows * n, transcendentals=0),
    )(x, *turns)


def arrived_kernel(place_ref, inner, outer, t_inner, *rest):
    t_outer, out, parts = rest[:PIECES], rest[-2], rest[-1]
    half = t_inner.shape[1]
    piece = t_inner.shape[0] // PIECES

    @pl.when(pl.program_id(0) == 0)
    def _():
        parts[0, 0], parts[0, 1] = split(t_inner[...])
        for d, t in enumerate(t_outer):
            at = pl.ds(pl.multiple_of((place_ref[1] + PIECES - d) % PIECES * piece, piece), piece)
            hi, lo = split(t[...])
            parts[1, 0, at] = hi
            parts[1, 1, at] = lo

    for side, block in enumerate((inner, outer)):
        at = pl.ds(pl.multiple_of(jnp.bitwise_xor(place_ref[0], 1 - side) * half, half), half)
        out[:, at] = dot3(split(block[...]), (parts[side, 0], parts[side, 1]))


def arrived_rows(out, shape, begin, rows, place, blocks, skip, turns):
    n = shape[1]
    tile = tile_for(begin, rows, skip)
    first, here = begin // tile, skip // tile
    args = [place, *blocks, *turns] + ([] if out is None else [out])
    return pl.pallas_call(
        arrived_kernel,
        grid=(rows // tile,),
        in_specs=[
            pl.BlockSpec(memory_space=pltpu.SMEM),
            pl.BlockSpec((tile, n), lambda i: (here + i, 0)),
            pl.BlockSpec((tile, n), lambda i: (here + i, 0)),
        ]
        + [pl.BlockSpec(t.shape, lambda i: (0, 0)) for t in turns]
        + [pl.BlockSpec(memory_space=pl.ANY)] * (out is not None),
        out_specs=pl.BlockSpec((tile, n), lambda i: (first + i, 0)),
        scratch_shapes=[pltpu.VMEM((2, 2, n, n // 2), BF16)],
        out_shape=jax.ShapeDtypeStruct(shape, F32),
        input_output_aliases={} if out is None else {len(args) - 1: 0},
        compiler_params=pltpu.CompilerParams(vmem_limit_bytes=24 * 2**20),
        cost_estimate=pl.CostEstimate(flops=6 * rows * n * n, bytes_accessed=8 * rows * n, transcendentals=0),
    )(*args)


def place_kernel(core_ref, inner, outer, *rest):
    out = rest[-1]
    half = inner.shape[1]
    for side, block in enumerate((inner, outer)):
        at = pl.ds(pl.multiple_of(jnp.bitwise_xor(core_ref[0], 1 - side) * half, half), half)
        out[:, at] = block[...]


def place_rows(out, shape, begin, core, blocks):
    rows, half = blocks[0].shape
    tile = tile_for(begin, rows)
    first = begin // tile
    args = [core, *blocks] + ([] if out is None else [out])
    return pl.pallas_call(
        place_kernel,
        grid=(rows // tile,),
        in_specs=[pl.BlockSpec(memory_space=pltpu.SMEM)]
        + [pl.BlockSpec((tile, half), lambda i: (i, 0))] * 2
        + [pl.BlockSpec(memory_space=pl.ANY)] * (len(args) - 3),
        out_specs=pl.BlockSpec((tile, 2 * half), lambda i: (first + i, 0)),
        out_shape=jax.ShapeDtypeStruct(shape, F32),
        input_output_aliases={} if out is None else {len(args) - 1: 0},
        compiler_params=pltpu.CompilerParams(vmem_limit_bytes=8 * 2**20),
        cost_estimate=pl.CostEstimate(flops=1024, bytes_accessed=16 * rows * half, transcendentals=0),
    )(*args)


EARLY = ((1, 0, 1024),)
LATE = ((0, 0, 1024), (0, 1024, 1024), (0, 2048, 1024), (0, 3072, 512))


def raw_rows(sources):
    blocks = [lax.slice_in_dim(sources[w], begin, begin + rows) for w, begin, rows in EARLY]
    return blocks[0] if len(blocks) == 1 else jnp.concatenate(blocks)


def on_device(matrix, vectors):
    count = lax.axis_size("col")
    own_index = lax.axis_index("col")
    core = jnp.reshape(own_index % 2, (1,)).astype(jnp.int32)
    within = [(i, i ^ 1) for i in range(count)]
    across = [(0, 0), (count - 1, count - 1)]
    across += [(i, i + 1) for i in range(1, count - 1, 2)] + [(i + 1, i) for i in range(1, count - 1, 2)]
    swap = jnp.where(own_index == 0, 1, core).astype(jnp.int32)
    sources = (matrix, vectors)
    results = [None, None]

    def pass_on(inner, outer):
        return lax.ppermute(inner, "col", within), lax.ppermute(outer, "col", across)

    count_row = lax.axis_size("row")
    ring = lax.axis_index("row") // (count_row // PIECES)
    place = jnp.concatenate([core, jnp.reshape(ring, (1,)).astype(jnp.int32)])

    gram = sum_over_rows(make_gram(matrix))
    raw, gram = lax.optimization_barrier((raw_rows(sources), gram))
    early = pass_on(raw, raw)
    own_turns = make_transform(gram, swap)
    piece = own_turns[1].shape[0] // PIECES
    t_inner = lax.ppermute(own_turns[0], "col", within)
    t_piece = lax.ppermute(lax.dynamic_slice_in_dim(own_turns[1], ring * piece, piece), "col", across)
    pieces, late = [t_piece], []
    for k, (which, begin, rows) in enumerate(LATE):
        inner, outer = apply_rows(sources[which], begin, rows, own_turns)
        if k < DEPTH:
            outer, pieces[0], early = lax.optimization_barrier((outer, pieces[0], early))
        else:
            outer, late[k - DEPTH][1] = lax.optimization_barrier((outer, late[k - DEPTH][1]))
        late.append(list(pass_on(inner, outer)))
    for d in range(1, PIECES):
        step = d * (count_row // PIECES)
        around = [(i, (i + step) % count_row) for i in range(count_row)]
        pieces.append(lax.ppermute(pieces[0], "row", around))
    turns = (t_inner, *pieces)
    skip = 0
    for which, begin, rows in EARLY:
        results[which] = arrived_rows(
            results[which], sources[which].shape, begin, rows, place, early, skip, turns
        )
        skip += rows
    for (which, begin, rows), blocks in zip(LATE, late):
        results[which] = place_rows(results[which], sources[which].shape, begin, core, blocks)
    return tuple(results)


def solution(mesh):
    in_specs = (P("row", "col"), P("row", "col"))
    out_specs = (P("row", "col"), P("row", "col"))
    return jax.shard_map(
        on_device, mesh=mesh, in_specs=in_specs, out_specs=out_specs, check_vma=False
    )
```

```python
import functools

import jax
import jax.numpy as jnp
from jax import lax
from jax.experimental import pallas as pl
from jax.experimental.pallas import tpu as pltpu
from jax.sharding import PartitionSpec as P

POLAR_STEPS = 10
LEAF = 128
VMEM_ALL = 60 * 2**20
BLOCKS = 4
UPPER = tuple((i, j) for i in range(BLOCKS) for j in range(i, BLOCKS))
PIECES = 4
DEPTH = 2
F32 = jnp.float32
BF16 = jnp.bfloat16
NT = (((1,), (1,)), ((), ()))
NN = (((1,), (0,)), ((), ()))
TN = (((0,), (0,)), ((), ()))


def split(x):
    hi = x.astype(BF16)
    return hi, (x - hi.astype(F32)).astype(BF16)


def dot3(a, b, dims=NN):
    dot = functools.partial(lax.dot_general, dimension_numbers=dims, preferred_element_type=F32)
    return dot(a[0], b[1]) + dot(a[1], b[0]) + dot(a[0], b[0])


def dot_high(a, b, dims=NN):
    return lax.dot_general(a, b, dims, precision=lax.Precision.HIGHEST, preferred_element_type=F32)


def eliminate_leaf(block):
    groups = LEAF // 8
    rows = [block[8 * g : 8 * g + 8, :] for g in range(groups)]
    inv_pivot = []
    lane = lax.broadcasted_iota(jnp.int32, (8, LEAF), 1)
    sub = lax.broadcasted_iota(jnp.int32, (8, LEAF), 0)
    for p in range(groups):
        j0 = 8 * p
        panel = rows[p]
        cols = [jnp.broadcast_to(panel[:, j0 + u : j0 + u + 1], (8, LEAF)) for u in range(8)]
        s = [[None] * 8 for _ in range(8)]
        for t in range(8):
            for u in range(t, 8):
                s[t][u] = jnp.broadcast_to(cols[u][t : t + 1, :], (8, LEAF))
        in_panel = (lane >= j0) & (lane < j0 + 8)
        unit = (lane - j0 == sub).astype(F32)
        panel = jnp.where(in_panel, unit, panel)
        line = [jnp.broadcast_to(panel[t : t + 1, :], (8, LEAF)) for t in range(8)]
        recip = []
        for t in range(8):
            r = 1.0 / s[t][t]
            recip.append(r)
            for u in range(t + 1, 8):
                f = s[t][u] * r
                for v in range(u, 8):
                    s[u][v] = s[u][v] - f * s[t][v]
                line[u] = line[u] - f * line[t]
        done = line[7]
        inv = recip[7]
        for t in range(6, -1, -1):
            done = jnp.where(sub == t, line[t], done)
            inv = jnp.where(sub == t, recip[t], inv)
        rows[p] = done
        inv_pivot.append(inv)
        for g in range(p + 1, groups):
            cur = rows[g]
            left = [jnp.broadcast_to(cur[:, j0 + u : j0 + u + 1], (8, LEAF)) for u in range(8)]
            cur = jnp.where(in_panel, 0.0, cur)
            for t in range(8):
                m = left[t] * recip[t]
                for u in range(t + 1, 8):
                    left[u] = left[u] - m * s[t][u]
                cur = cur - m * line[t]
            rows[g] = cur
    return jnp.concatenate(rows, axis=0), jnp.concatenate(inv_pivot, axis=0)


def gram_kernel(cuts, x_hbm, out_ref, x, same, cross, sems):
    half = x.shape[1] // 2
    copies = []
    for k, (begin, end) in enumerate(zip(cuts[:-1], cuts[1:])):
        at = pl.ds(begin, end - begin)
        copies.append(pltpu.make_async_copy(x_hbm.at[at], x.at[at], sems.at[k]))
        copies[-1].start()
    dot = functools.partial(lax.dot_general, dimension_numbers=TN, preferred_element_type=F32)
    for k, (begin, end) in enumerate(zip(cuts[:-1], cuts[1:])):
        copies[k].wait()
        hi, lo = split(x[begin:end])
        first, last, mixed = dot(hi[:, :half], hi), dot(hi[:, half:], hi[:, half:]), dot(hi, lo)
        if k == 0:
            same[:half, :] = first
            same[half:, half:] = last
            cross[...] = mixed
        else:
            same[:half, :] += first
            same[half:, half:] += last
            cross[...] += mixed
    for k, (i, j) in enumerate(UPPER):
        rows, cols = slice(i * LEAF, (i + 1) * LEAF), slice(j * LEAF, (j + 1) * LEAF)
        out_ref[k * LEAF : (k + 1) * LEAF] = same[rows, cols] + (cross[rows, cols] + cross[cols, rows].T)


def make_gram(x):
    rows, n = x.shape
    size = (len(UPPER) * LEAF, LEAF)
    cuts = (0, rows // 7, 3 * rows // 7, rows)
    return pl.pallas_call(
        functools.partial(gram_kernel, cuts),
        out_shape=jax.ShapeDtypeStruct(size, F32),
        in_specs=[pl.BlockSpec(memory_space=pl.ANY)],
        out_specs=pl.BlockSpec(memory_space=pltpu.VMEM),
        scratch_shapes=[
            pltpu.VMEM((rows, n), F32),
            pltpu.VMEM((n, n), F32),
            pltpu.VMEM((n, n), F32),
            pltpu.SemaphoreType.DMA((len(cuts) - 1,)),
        ],
        compiler_params=pltpu.CompilerParams(vmem_limit_bytes=VMEM_ALL),
        cost_estimate=pl.CostEstimate(flops=1024, bytes_accessed=1024, transcendentals=0),
    )(x)


def add_kernel(pieces, out_ref):
    total = pieces[0]
    for k in range(1, pieces.shape[0]):
        total = total + pieces[k]
    for k in range(pieces.shape[0]):
        out_ref[k] = total


def sum_over_rows(gram):
    count = lax.axis_size("row")
    pieces = gram.reshape(count, gram.shape[0] // count, gram.shape[1])
    theirs = lax.all_to_all(pieces, "row", 0, 0, tiled=True)
    spread = pl.pallas_call(
        add_kernel,
        out_shape=jax.ShapeDtypeStruct(pieces.shape, F32),
        in_specs=[pl.BlockSpec(memory_space=pltpu.VMEM)],
        out_specs=pl.BlockSpec(memory_space=pltpu.VMEM),
        compiler_params=pltpu.CompilerParams(vmem_limit_bytes=8 * 2**20),
        cost_estimate=pl.CostEstimate(flops=1024, bytes_accessed=1024, transcendentals=0),
    )(theirs)
    return lax.all_to_all(spread, "row", 0, 0, tiled=True).reshape(gram.shape)


def transform_kernel(swap_ref, gram_ref, inner_ref, outer_ref, work, gram):
    n = work.shape[0]
    half = n // 2
    for k, (i, j) in enumerate(UPPER):
        block = gram_ref[k * LEAF : (k + 1) * LEAF]
        work[i * LEAF : (i + 1) * LEAF, j * LEAF : (j + 1) * LEAF] = block
        if i != j:
            work[j * LEAF : (j + 1) * LEAF, i * LEAF : (i + 1) * LEAF] = block.T

    def block_step(p, carry):
        at = pl.ds(pl.multiple_of(p * LEAF, LEAF), LEAF)
        block, inv = eliminate_leaf(work[at, at])
        r = lax.broadcasted_iota(jnp.int32, (LEAF, LEAF), 0)
        c = lax.broadcasted_iota(jnp.int32, (LEAF, LEAF), 1)
        lower = jnp.where(c <= r, block, 0.0)
        work[at, at] = (r == c).astype(F32)
        for q in range(n // LEAF):

            @pl.when(p == q)
            def _():
                e = (q + 1) * LEAF
                panel = dot_high(lower, work[q * LEAF : e, :])
                work[q * LEAF : e, :] = panel
                if e < n:
                    scaled = panel[:, e:] * inv[:, :1]
                    work[e:, q * LEAF : e] = jnp.zeros((n - e, LEAF), F32)
                    work[e:, :] -= dot_high(scaled, panel, TN)

        return carry

    lax.fori_loop(0, n // LEAF, block_step, 0)
    r = lax.broadcasted_iota(jnp.int32, (n, n), 0)
    c = lax.broadcasted_iota(jnp.int32, (n, n), 1)
    start = jnp.where(c <= r, work[...], 0.0)
    mag = jnp.abs(start)
    bound = jnp.sqrt(jnp.max(jnp.sum(mag, axis=0, keepdims=True)) * jnp.max(jnp.sum(mag, axis=1, keepdims=True)))
    work[...] = start / bound

    def polar_step(k, carry):
        z = work[...]
        zs = split(z)
        top = tuple(part[:half] for part in zs)
        low = tuple(part[half:] for part in zs)
        upper = dot3(top, zs, NT)
        gram[:half, :] = upper
        gram[half:, :half] = upper[:, half:].T
        gram[half:, half:] = dot3(low, low, NT)
        work[...] = 1.5 * z - 0.5 * dot3(split(gram[...]), zs)
        return carry

    lax.fori_loop(0, POLAR_STEPS, polar_step, 0)
    for side, out in enumerate((inner_ref, outer_ref)):
        begin = pl.multiple_of(jnp.bitwise_xor(swap_ref[0], side) * half, half)
        out[...] = work[pl.ds(begin, half), :].T


def make_transform(gram, swap):
    n = BLOCKS * LEAF
    return pl.pallas_call(
        transform_kernel,
        out_shape=[jax.ShapeDtypeStruct((n, n // 2), F32)] * 2,
        in_specs=[pl.BlockSpec(memory_space=pltpu.SMEM), pl.BlockSpec(memory_space=pltpu.VMEM)],
        out_specs=[pl.BlockSpec(memory_space=pltpu.VMEM)] * 2,
        scratch_shapes=[pltpu.VMEM((n, n), F32)] * 2,
        compiler_params=pltpu.CompilerParams(vmem_limit_bytes=16 * 2**20),
        cost_estimate=pl.CostEstimate(flops=1024, bytes_accessed=1024, transcendentals=0),
    )(swap, gram)


def tile_for(*extents):
    return 512 if all(e % 512 == 0 for e in extents) else 256


def apply_kernel(x_ref, t_inner, t_outer, inner_ref, outer_ref, parts):
    half = inner_ref.shape[1]

    @pl.when(pl.program_id(0) == 0)
    def _():
        for side, t in enumerate((t_inner, t_outer)):
            hi, lo = split(t[...])
            parts[0, :, side * half : (side + 1) * half] = hi
            parts[1, :, side * half : (side + 1) * half] = lo

    both = dot3(split(x_ref[...]), (parts[0], parts[1]))
    inner_ref[...] = both[:, :half]
    outer_ref[...] = both[:, half:]


def apply_rows(x, begin, rows, turns):
    tile = tile_for(begin, rows)
    n = x.shape[1]
    half = n // 2
    first = begin // tile
    return pl.pallas_call(
        apply_kernel,
        grid=(rows // tile,),
        out_shape=[jax.ShapeDtypeStruct((rows, half), F32)] * 2,
        in_specs=[
            pl.BlockSpec((tile, n), lambda i: (first + i, 0)),
            pl.BlockSpec((n, half), lambda i: (0, 0)),
            pl.BlockSpec((n, half), lambda i: (0, 0)),
        ],
        out_specs=[pl.BlockSpec((tile, half), lambda i: (i, 0))] * 2,
        scratch_shapes=[pltpu.VMEM((2, n, n), BF16)],
        compiler_params=pltpu.CompilerParams(vmem_limit_bytes=14 * 2**20),
        cost_estimate=pl.CostEstimate(flops=6 * rows * n * n, bytes_accessed=8 * rows * n, transcendentals=0),
    )(x, *turns)


def arrived_kernel(place_ref, inner, outer, t_inner, *rest):
    t_outer, out, parts = rest[:PIECES], rest[-2], rest[-1]
    half = t_inner.shape[1]
    piece = t_inner.shape[0] // PIECES

    @pl.when(pl.program_id(0) == 0)
    def _():
        parts[0, 0], parts[0, 1] = split(t_inner[...])
        for d, t in enumerate(t_outer):
            at = pl.ds(pl.multiple_of((place_ref[1] + PIECES - d) % PIECES * piece, piece), piece)
            hi, lo = split(t[...])
            parts[1, 0, at] = hi
            parts[1, 1, at] = lo

    for side, block in enumerate((inner, outer)):
        at = pl.ds(pl.multiple_of(jnp.bitwise_xor(place_ref[0], 1 - side) * half, half), half)
        out[:, at] = dot3(split(block[...]), (parts[side, 0], parts[side, 1]))


def arrived_rows(out, shape, begin, rows, place, blocks, skip, turns):
    n = shape[1]
    tile = tile_for(begin, rows, skip)
    first, here = begin // tile, skip // tile
    args = [place, *blocks, *turns] + ([] if out is None else [out])
    return pl.pallas_call(
        arrived_kernel,
        grid=(rows // tile,),
        in_specs=[
            pl.BlockSpec(memory_space=pltpu.SMEM),
            pl.BlockSpec((tile, n), lambda i: (here + i, 0)),
            pl.BlockSpec((tile, n), lambda i: (here + i, 0)),
        ]
        + [pl.BlockSpec(t.shape, lambda i: (0, 0)) for t in turns]
        + [pl.BlockSpec(memory_space=pl.ANY)] * (out is not None),
        out_specs=pl.BlockSpec((tile, n), lambda i: (first + i, 0)),
        scratch_shapes=[pltpu.VMEM((2, 2, n, n // 2), BF16)],
        out_shape=jax.ShapeDtypeStruct(shape, F32),
        input_output_aliases={} if out is None else {len(args) - 1: 0},
        compiler_params=pltpu.CompilerParams(vmem_limit_bytes=24 * 2**20),
        cost_estimate=pl.CostEstimate(flops=6 * rows * n * n, bytes_accessed=8 * rows * n, transcendentals=0),
    )(*args)


def place_kernel(core_ref, inner, outer, *rest):
    out = rest[-1]
    half = inner.shape[1]
    for side, block in enumerate((inner, outer)):
        at = pl.ds(pl.multiple_of(jnp.bitwise_xor(core_ref[0], 1 - side) * half, half), half)
        out[:, at] = block[...]


def place_rows(out, shape, begin, core, blocks):
    rows, half = blocks[0].shape
    tile = tile_for(begin, rows)
    first = begin // tile
    args = [core, *blocks] + ([] if out is None else [out])
    return pl.pallas_call(
        place_kernel,
        grid=(rows // tile,),
        in_specs=[pl.BlockSpec(memory_space=pltpu.SMEM)]
        + [pl.BlockSpec((tile, half), lambda i: (i, 0))] * 2
        + [pl.BlockSpec(memory_space=pl.ANY)] * (len(args) - 3),
        out_specs=pl.BlockSpec((tile, 2 * half), lambda i: (first + i, 0)),
        out_shape=jax.ShapeDtypeStruct(shape, F32),
        input_output_aliases={} if out is None else {len(args) - 1: 0},
        compiler_params=pltpu.CompilerParams(vmem_limit_bytes=8 * 2**20),
        cost_estimate=pl.CostEstimate(flops=1024, bytes_accessed=16 * rows * half, transcendentals=0),
    )(*args)


EARLY = ((1, 0, 1024),)
LATE = ((0, 0, 1024), (0, 1024, 1024), (0, 2048, 1024), (0, 3072, 512))


def raw_rows(sources):
    blocks = [lax.slice_in_dim(sources[w], begin, begin + rows) for w, begin, rows in EARLY]
    return blocks[0] if len(blocks) == 1 else jnp.concatenate(blocks)


def on_device(matrix, vectors):
    count = lax.axis_size("col")
    own_index = lax.axis_index("col")
    core = jnp.reshape(own_index % 2, (1,)).astype(jnp.int32)
    within = [(i, i ^ 1) for i in range(count)]
    across = [(0, 0), (count - 1, count - 1)]
    across += [(i, i + 1) for i in range(1, count - 1, 2)] + [(i + 1, i) for i in range(1, count - 1, 2)]
    swap = jnp.where(own_index == 0, 1, core).astype(jnp.int32)
    sources = (matrix, vectors)
    results = [None, None]

    def pass_on(inner, outer):
        return lax.ppermute(inner, "col", within), lax.ppermute(outer, "col", across)

    count_row = lax.axis_size("row")
    ring = lax.axis_index("row") // (count_row // PIECES)
    place = jnp.concatenate([core, jnp.reshape(ring, (1,)).astype(jnp.int32)])

    gram = sum_over_rows(make_gram(matrix))
    raw, gram = lax.optimization_barrier((raw_rows(sources), gram))
    early = pass_on(raw, raw)
    own_turns = make_transform(gram, swap)
    piece = own_turns[1].shape[0] // PIECES
    t_inner = lax.ppermute(own_turns[0], "col", within)
    t_piece = lax.ppermute(lax.dynamic_slice_in_dim(own_turns[1], ring * piece, piece), "col", across)
    pieces, late = [t_piece], []
    for k, (which, begin, rows) in enumerate(LATE):
        inner, outer = apply_rows(sources[which], begin, rows, own_turns)
        if k < DEPTH:
            outer, pieces[0], early = lax.optimization_barrier((outer, pieces[0], early))
        else:
            outer, late[k - DEPTH][1] = lax.optimization_barrier((outer, late[k - DEPTH][1]))
        late.append(list(pass_on(inner, outer)))
    for d in range(1, PIECES):
        step = d * (count_row // PIECES)
        around = [(i, (i + step) % count_row) for i in range(count_row)]
        pieces.append(lax.ppermute(pieces[0], "row", around))
    turns = (t_inner, *pieces)
    skip = 0
    for which, begin, rows in EARLY:
        results[which] = arrived_rows(
            results[which], sources[which].shape, begin, rows, place, early, skip, turns
        )
        skip += rows
    for (which, begin, rows), blocks in zip(LATE, late):
        results[which] = place_rows(results[which], sources[which].shape, begin, core, blocks)
    return tuple(results)


def solution(mesh):
    in_specs = (P("row", "col"), P("row", "col"))
    out_specs = (P("row", "col"), P("row", "col"))
    return jax.shard_map(
        on_device, mesh=mesh, in_specs=in_specs, out_specs=out_specs, check_vma=False
    )
```
